32 devices in a mesh: ch: 8 (over y, x, core), ta: 4 (over z).
Axes of the slice: x: 2, y: 2, z: 4, core: 2. Of those that a mesh axis runs over, the one named last changes fastest.
Arguments:
- samples: float32 [256, 8192], P('ch', 'ta'), may hold values from -80 to 80
- dead_mask: int32 [256], P('ch'), may hold values 0 or 1
- owners: int32 [2], replicated, may hold values from 0 to 7
Outputs:
- correlation: float32 [2, 32, 256, 128], P(None, None, 'ch', 'ta')
The draws below stay inside these ranges and needn't reach their ends.
All inputs are finite; a program needn't handle non-finite values. No bound on the sum of `dead_mask` on one device may be relied on, other than what follows from the above.
Results may differ from the reference program's by a relative error of at most 0.0036.
Values may be sent and summed in bfloat16 or wider, within the bound.
No kernel may reach another device: no remote copies, remote signals or barrier semaphores. Data moves between devices by JAX's collectives and lax.ppermute only.
A program may use at most 64 MiB of HBM per device.

```python
import math
import jax
import jax.numpy as jnp
from jax import lax

CH_DEV = 32
NT = 8192
NBINS = 4096
W = 32
LAGS = 128
STEPS = 2
CHANNELS = 256
N_CH = 8


def draw_samples(key, part):
    key = jax.random.fold_in(key, 11)
    scale_key, noise_key = jax.random.split(key, 2)
    scales = jnp.exp(jax.random.uniform(scale_key, (CHANNELS, 1, 1), jnp.float32, 0.0, math.log(10.0)))
    noise = jnp.clip(jax.random.normal(noise_key, (CHANNELS, 32, NT // 32), jnp.float32), -6.0, 6.0)
    values = noise * scales
    return values.reshape(CHANNELS, NT).astype(jnp.float32)


def touch_ends(result, rng, smallest, largest):
    place = [jax.random.randint(jax.random.fold_in(rng, axis), (), 0, length) for axis, length in enumerate(result.shape)]
    widest = result.shape.index(max(result.shape))
    beside = place[:widest] + [(place[widest] + 1) % result.shape[widest]] + place[widest + 1:]
    return result.at[tuple(place)].set(smallest).at[tuple(beside)].set(largest)


def setup_inputs(seed: int = 0) -> dict:
    seeds = jax.random.split(jax.random.key(seed), 4)
    samples = draw_samples(jax.random.fold_in(seeds[3], 71), 0)
    dead_mask = touch_ends((jax.random.randint(seeds[1], (CHANNELS,), 0, 8) < 7).astype(jnp.int32), jax.random.fold_in(seeds[1], 1), 0, 1)
    owners = jax.random.randint(seeds[2], (STEPS,), 0, N_CH).astype(jnp.int32)
    return dict(samples=samples, dead_mask=dead_mask, owners=owners)


epsilon = 1e-06

def phases(first_index, second_index, period):
    turn_count = first_index[:, None] * second_index[None, :] % period
    angles = turn_count.astype(jnp.float32) * (2.0 * math.pi / period)
    return (jnp.cos(angles), jnp.sin(angles))

def reference(samples, dead_mask, owners):
    spectrum = jnp.fft.rfft(samples, axis=1)[:, :NBINS]
    spec_real = jnp.real(spectrum).astype(jnp.float32)
    spec_imag = jnp.imag(spectrum).astype(jnp.float32)
    amplitude = jnp.sqrt(spec_real * spec_real + spec_imag * spec_imag)
    padded = jnp.pad(amplitude, ((0, 0), (W, W)))
    window = padded[:, 0:NBINS]
    for offset_index in range(1, 2 * W + 1):
        window = window + padded[:, offset_index:offset_index + NBINS]
    smooth = window / (2 * W + 1)
    alive_mask = dead_mask.astype(jnp.float32)[:, None]
    divisor = smooth + epsilon
    whitened = jnp.stack([spec_real / divisor * alive_mask, spec_imag / divisor * alive_mask]).astype(jnp.bfloat16)
    panels = jnp.stack([lax.dynamic_slice_in_dim(whitened, (owners[step_index] * CH_DEV).astype(jnp.int32), CH_DEV, 1) for step_index in range(STEPS)])
    panel_values = panels.astype(jnp.float32)
    frequency = jnp.arange(NBINS, dtype=jnp.int32)
    lag_turns = (jnp.arange(LAGS, dtype=jnp.int32) - LAGS // 2) % NT
    lag_cos, lag_sin = phases(frequency, lag_turns, NT)

    def one_block(block_index):
        resident = lax.dynamic_slice_in_dim(whitened, (block_index * CH_DEV).astype(jnp.int32), CH_DEV, 1).astype(jnp.float32)
        res_real = resident[0].T[:, :, None]
        res_imag = resident[1].T[:, :, None]
        first_half = res_real * lag_cos[:, None, :] + res_imag * lag_sin[:, None, :]
        second = res_imag * lag_cos[:, None, :] - res_real * lag_sin[:, None, :]
        kernel = jnp.stack([first_half, second]).reshape(2, NBINS, CH_DEV * LAGS)
        product = lax.dot_general(panel_values, kernel, (((1, 3), (0, 1)), ((), ())), precision=lax.Precision.HIGHEST, preferred_element_type=jnp.float32)
        return product.reshape(STEPS, CH_DEV, CH_DEV, LAGS)
    blocks = lax.map(one_block, jnp.arange(N_CH, dtype=jnp.int32))
    correlation = blocks.transpose(1, 2, 0, 3, 4).reshape(STEPS, CH_DEV, CHANNELS, LAGS)
    return correlation * (1.0 / math.sqrt(NBINS))
```

```python
import math

import jax
import jax.numpy as jnp
import numpy as np
from jax import lax
from jax.experimental import pallas as pl
from jax.experimental.pallas import tpu as pltpu
from jax.sharding import PartitionSpec as P

NT = 8192
BINS = NT // 2
W = 32
LAGS = 128
EPS = 1e-06

N1 = 32
N2 = 256
K2 = BINS // N1
assert N1 == W and K2 == 128


def split_bf16(x):
    high = x.astype(jnp.bfloat16)
    low = (x - high.astype(jnp.float32)).astype(jnp.bfloat16)
    return high, low


def twiddle_tables():
    angle = 2.0 * np.pi * (np.outer(np.arange(N1), np.arange(N2)) % NT) / NT
    return np.cos(angle).astype(np.float32), np.sin(angle).astype(np.float32)


def column_tables():
    angle = 2.0 * np.pi * (np.outer(np.arange(N2), np.arange(K2)) % N2) / N2
    cos, sin = np.cos(angle), np.sin(angle)
    table = np.block([[cos, -sin], [sin, cos]])
    high = table.astype(jnp.bfloat16)
    low = (table - high.astype(np.float64)).astype(jnp.bfloat16)
    return high, low


def lag_table():
    k = np.arange(N1)[:, None] + N1 * np.arange(K2)[None, :]
    turns = (k[:, :, None] * ((np.arange(LAGS) - LAGS // 2) % NT)) % NT
    angle = 2.0 * np.pi * turns / NT
    table = np.stack([np.cos(angle), np.sin(angle)], axis=1) / math.sqrt(BINS)
    return table.reshape(N1 * 2 * K2, LAGS).astype(jnp.bfloat16)


def add(x, y):
    return y if x is None else x if y is None else x + y


def sub(x, y):
    return (None if y is None else -y) if x is None else x if y is None else x - y


def times(z, turn):
    re, im = z
    turn = turn % 1.0
    if turn == 0.0:
        return z
    if turn == 0.25:
        return im, None if re is None else -re
    cos, sin = math.cos(2 * math.pi * turn), math.sin(2 * math.pi * turn)
    if im is None:
        return re * cos, re * -sin
    return re * cos + im * sin, im * cos - re * sin


def real_fft(xs):
    n = len(xs)
    if n == 1:
        return [(xs[0], None)]
    if n == 2:
        return [(xs[0] + xs[1], None), (xs[0] - xs[1], None)]
    even, odd = real_fft(xs[0::2]), real_fft(xs[1::2])
    half = n // 2
    out = [None] * (half + 1)
    for k in range(half // 2 + 1):
        e, o = even[k], times(odd[k], k / n)
        out[k] = (add(e[0], o[0]), add(e[1], o[1]))
        re, im = sub(e[0], o[0]), sub(o[1], e[1])
        if k != half - k:
            out[half - k] = (re, im)
    return out


def spectrum_kernel(
    tparts, samples, *rest
):
    blocks = rest[: tparts - 1]
    mask, cos, sin, high, low, out, series, rows, spec = rest[tparts - 1 :]
    me = lax.axis_index("ta")
    channels = out.shape[1] // 2
    series[me] = samples[pl.ds(pl.multiple_of(me * channels, channels), channels), :]
    for step in range(1, tparts):
        series[me ^ step] = blocks[step - 1][...]
    per_part = N1 // tparts
    for start in range(0, N2, 128):
        lanes = slice(start, start + 128)
        xs = [
            series[a // per_part, :, pl.ds((a % per_part) * N2 + start, 128)] for a in range(N1)
        ]
        bins = real_fft(xs)
        for k1 in range(N1):
            if k1 <= N1 // 2:
                re, im = bins[k1]
            else:
                re, im = bins[N1 - k1]
                im = -im
            c, s = cos[k1 : k1 + 1, lanes], sin[k1 : k1 + 1, lanes]
            if im is None:
                new = re * c, -re * s
            else:
                new = re * c + im * s, im * c - re * s
            at = slice(k1 * channels, (k1 + 1) * channels)
            rows[at, start : start + 128] = new[0]
            rows[at, N2 + start : N2 + start + 128] = new[1]
    chunk = 128
    for start in range(0, N1 * channels, chunk):
        left, left_low = split_bf16(rows[start : start + chunk, :])
        total = jnp.dot(left, high[...], preferred_element_type=jnp.float32)
        total += jnp.dot(left_low, high[...], preferred_element_type=jnp.float32)
        total += jnp.dot(left, low[...], preferred_element_type=jnp.float32)
        spec[start : start + chunk, :] = total

    def parts(k1):
        at = slice(k1 * channels, (k1 + 1) * channels)
        return spec[at, :K2], spec[at, K2:]

    amplitude = []
    for k1 in range(N1):
        re, im = parts(k1)
        amplitude.append(jnp.sqrt(re * re + im * im))
    suffix = [None] * N1
    running = None
    for k1 in reversed(range(N1)):
        running = add(running, amplitude[k1])
        suffix[k1] = running
    column = running
    lane = lax.broadcasted_iota(jnp.int32, (channels, K2), 1)
    row = lax.broadcasted_iota(jnp.int32, (channels, K2), 0)
    alive = jnp.zeros((channels, K2), jnp.float32)
    for c in range(channels):
        alive = jnp.where(row == c, mask[me * channels + c].astype(jnp.float32), alive)
    prefix = None
    for k1 in range(N1):
        prefix = add(prefix, amplitude[k1])
        above = jnp.where(lane == K2 - 1, 0.0, pltpu.roll(prefix, K2 - 1, 1))
        below = jnp.where(lane == 0, 0.0, pltpu.roll(suffix[k1], 1, 1))
        divisor = (column + above + below) / (2 * W + 1) + EPS
        scale = alive / divisor
        re, im = parts(k1)
        out[k1] = jnp.concatenate([re * scale, im * scale], axis=0).astype(jnp.bfloat16)


def spectrum(samples, blocks, dead_mask):
    tparts = lax.axis_size("ta")
    channels = samples.shape[0] // tparts
    cos, sin = twiddle_tables()
    high, low = column_tables()
    vmem = pl.BlockSpec(memory_space=pltpu.VMEM)
    smem = pl.BlockSpec(memory_space=pltpu.SMEM)
    return pl.pallas_call(
        lambda *refs: spectrum_kernel(tparts, *refs),
        out_shape=jax.ShapeDtypeStruct((N1, 2 * channels, K2), jnp.bfloat16),
        in_specs=[vmem] * tparts + [smem] + [vmem] * 4,
        out_specs=vmem,
        scratch_shapes=[
            pltpu.VMEM((tparts, channels, samples.shape[1]), jnp.float32),
            pltpu.VMEM((N1 * channels, 2 * N2), jnp.float32),
            pltpu.VMEM((N1 * channels, 2 * K2), jnp.float32),
        ],
        compiler_params=pltpu.CompilerParams(vmem_limit_bytes=32 * 1024 * 1024),
        cost_estimate=pl.CostEstimate(flops=10**9, bytes_accessed=10**6, transcendentals=10**5),
        name="spectrum",
    )(samples, *blocks, dead_mask, cos, sin, high, low)


GROUP = 4


def correlate_kernel(tparts, panels, *rest):
    residents = rest[:tparts]
    table = rest[tparts]
    outs = rest[tparts + 1 : 2 * tparts + 1]
    cross, total = rest[2 * tparts + 1 :]
    steps, _, rows2, _ = panels.shape
    channels = rows2 // 2
    local = tparts * channels
    me = lax.axis_index("ta")
    total[...] = jnp.zeros_like(total)

    @pl.loop(0, N1 // GROUP)
    def _(group):
        for sub_index in range(GROUP):
            k1 = group * GROUP + sub_index
            col = sub_index * 2 * K2
            res = [r[k1].astype(jnp.float32) for r in residents]
            for s in range(steps):
                panel = panels[s, k1].astype(jnp.float32)
                for i in range(channels):
                    a = jnp.broadcast_to(panel[i : i + 1, :], (channels, K2))
                    b = jnp.broadcast_to(panel[channels + i : channels + i + 1, :], (channels, K2))
                    re, im = [], []
                    for value in res:
                        c, d = value[:channels], value[channels:]
                        re.append(a * c + b * d)
                        im.append(a * d - b * c)
                    at = pl.ds((s * channels + i) * local, local)
                    cross[at, pl.ds(col, K2)] = jnp.concatenate(re, axis=0).astype(jnp.bfloat16)
                    cross[at, pl.ds(col + K2, K2)] = jnp.concatenate(im, axis=0).astype(jnp.bfloat16)
        depth = GROUP * 2 * K2
        total[...] += jnp.dot(
            cross[...],
            table[pl.ds(pl.multiple_of(group * depth, depth), depth), :],
            preferred_element_type=jnp.float32,
        )

    width = LAGS // tparts
    lane = lax.broadcasted_iota(jnp.int32, (channels, LAGS), 1) // width
    for source in range(steps * channels):
        pieces = [
            total[source * local + step * channels : source * local + (step + 1) * channels, :]
            for step in range(tparts)
        ]
        for far in range(tparts):
            dest = me ^ far
            value = None
            for step in range(tparts):
                moved = pltpu.roll(pieces[step], (step - dest + tparts) * width % LAGS, 1)
                value = moved if value is None else jnp.where(lane == step, moved, value)
            outs[far][source * channels : (source + 1) * channels, :] = value.astype(outs[far].dtype)


def correlate(panels, residents):
    tparts = lax.axis_size("ta")
    steps, _, rows2, _ = panels.shape
    channels = rows2 // 2
    vmem = pl.BlockSpec(memory_space=pltpu.VMEM)
    pairs = steps * channels * channels * tparts
    return pl.pallas_call(
        lambda *refs: correlate_kernel(tparts, *refs),
        out_shape=[
            jax.ShapeDtypeStruct((steps * channels * channels, LAGS), jnp.float32)
        ] * tparts,
        in_specs=[vmem] * (tparts + 2),
        out_specs=[vmem] * tparts,
        scratch_shapes=[
            pltpu.VMEM((pairs, GROUP * 2 * K2), jnp.bfloat16),
            pltpu.VMEM((pairs, LAGS), jnp.float32),
        ],
        compiler_params=pltpu.CompilerParams(vmem_limit_bytes=32 * 1024 * 1024),
        cost_estimate=pl.CostEstimate(flops=4 * 10**9, bytes_accessed=3 * 10**6, transcendentals=0),
        name="correlate",
    )(panels, *residents, lag_table())


def place_kernel(tparts, steps, channels, *refs):
    pieces, out = refs[:tparts], refs[tparts]
    me = lax.axis_index("ta")
    width = LAGS // tparts
    for far in range(tparts):
        source = me ^ far
        value = pieces[far][...].astype(jnp.float32)
        for step in range(tparts):
            block = source ^ step
            moved = value if step == 0 else pltpu.roll(value, LAGS - step * width, 1)
            moved = moved[:, :width].reshape(steps, channels, channels, width)
            out[
                :,
                pl.ds(source * channels, channels),
                pl.ds(pl.multiple_of(block * channels, channels), channels),
                :,
            ] = moved


def place(pieces, steps, channels):
    tparts = lax.axis_size("ta")
    vmem = pl.BlockSpec(memory_space=pltpu.VMEM)
    local = tparts * channels
    return pl.pallas_call(
        lambda *refs: place_kernel(tparts, steps, channels, *refs),
        out_shape=jax.ShapeDtypeStruct((steps, local, local, LAGS // tparts), jnp.float32),
        in_specs=[vmem] * tparts,
        out_specs=vmem,
        compiler_params=pltpu.CompilerParams(vmem_limit_bytes=32 * 1024 * 1024),
        name="place",
    )(*pieces)


def flip(axis, mask):
    return [(i, i ^ mask) for i in range(lax.axis_size(axis))]


def owner_panels(block, owners):
    count = lax.axis_size("ch")
    steps = owners.shape[0]
    if count & (count - 1):
        return jnp.take(lax.all_gather(block, "ch"), owners, axis=0)
    me = lax.axis_index("ch")
    if count == 1:
        return jnp.stack([block] * steps)
    away = owners ^ me
    shape = (steps,) + (1,) * block.ndim
    other = lax.ppermute(block, "ch", flip("ch", 1))
    held = jnp.where(((away & 1) != 0).reshape(shape), other[None], block[None])
    masks = [1 << bit for bit in range(1, count.bit_length() - 1)]
    for even, odd in zip(masks, reversed(masks)):
        perm = [(i, i ^ (odd if i & 1 else even)) for i in range(count)]
        mask = jnp.where(me & 1, odd, even)
        other = lax.ppermute(held, "ch", perm)
        held = jnp.where(((away & mask) != 0).reshape(shape), other, held)
    return held


def body(samples, dead_mask, owners):
    tparts = lax.axis_size("ta")
    me = lax.axis_index("ta")
    channels = samples.shape[0] // tparts
    steps = owners.shape[0]

    def rows_for(part):
        return lax.dynamic_slice_in_dim(samples, part * channels, channels, 0)

    blocks = [
        lax.ppermute(rows_for(me ^ far), "ta", flip("ta", far)) for far in range(1, tparts)
    ]
    whitened = spectrum(samples, blocks, dead_mask)
    panels = owner_panels(whitened, owners)
    residents = [whitened] + [
        lax.ppermute(whitened, "ta", flip("ta", far)) for far in range(1, tparts)
    ]
    pieces = correlate(panels, residents)
    pieces = [pieces[0]] + [
        lax.ppermute(pieces[far], "ta", flip("ta", far)) for far in range(1, tparts)
    ]
    return place(pieces, steps, channels)


def solution(mesh):
    return jax.shard_map(
        body,
        mesh=mesh,
        in_specs=(P("ch", "ta"), P("ch"), P()),
        out_specs=P(None, None, "ch", "ta"),
        check_vma=False,
    )
```

```python
import math

import jax
import jax.numpy as jnp
import numpy as np
from jax import lax
from jax.experimental import pallas as pl
from jax.experimental.pallas import tpu as pltpu
from jax.sharding import PartitionSpec as P

NT = 8192
BINS = NT // 2
W = 32
LAGS = 128
EPS = 1e-06

N1 = 32
N2 = 256
K2 = BINS // N1
assert N1 == W and K2 == 128


def split_bf16(x):
    high = x.astype(jnp.bfloat16)
    low = (x - high.astype(jnp.float32)).astype(jnp.bfloat16)
    return high, low


def fft_tables():
    twiddle = 2.0 * np.pi * (np.outer(np.arange(N1), np.arange(N2)) % NT) / NT
    angle = 2.0 * np.pi * (np.outer(np.arange(N2), np.arange(K2)) % N2) / N2
    cos, sin = np.cos(angle), np.sin(angle)
    columns = np.block([[cos, -sin], [sin, cos]])
    return np.concatenate([np.cos(twiddle), np.sin(twiddle), columns]).astype(np.float32)


def lag_table():
    k = np.arange(N1)[:, None] + N1 * np.arange(K2)[None, :]
    turns = (k[:, :, None] * ((np.arange(LAGS) - LAGS // 2) % NT)) % NT
    angle = 2.0 * np.pi * turns / NT
    table = np.stack([np.cos(angle), np.sin(angle)], axis=1) / math.sqrt(BINS)
    return table.reshape(N1 * 2 * K2, LAGS).astype(jnp.bfloat16)


def add(x, y):
    return y if x is None else x if y is None else x + y


def sub(x, y):
    return (None if y is None else -y) if x is None else x if y is None else x - y


def times(z, turn):
    re, im = z
    turn = turn % 1.0
    if turn == 0.0:
        return z
    if turn == 0.25:
        return im, None if re is None else -re
    cos, sin = math.cos(2 * math.pi * turn), math.sin(2 * math.pi * turn)
    if im is None:
        return re * cos, re * -sin
    return re * cos + im * sin, im * cos - re * sin


def real_fft(xs):
    n = len(xs)
    if n == 1:
        return [(xs[0], None)]
    if n == 2:
        return [(xs[0] + xs[1], None), (xs[0] - xs[1], None)]
    even, odd = real_fft(xs[0::2]), real_fft(xs[1::2])
    half = n // 2
    out = [None] * (half + 1)
    for k in range(half // 2 + 1):
        e, o = even[k], times(odd[k], k / n)
        out[k] = (add(e[0], o[0]), add(e[1], o[1]))
        re, im = sub(e[0], o[0]), sub(o[1], e[1])
        if k != half - k:
            out[half - k] = (re, im)
    return out


def spectrum_kernel(tparts, *rest):
    blocks = rest[:tparts]
    alive, tables, out, series, rows, spec, high, low = rest[tparts:]
    me = lax.axis_index("ta")
    channels = out.shape[1] // 2
    for step in range(tparts):
        series[me ^ step] = blocks[step][...]
    high[...], low[...] = split_bf16(tables[2 * N1 :, :])
    per_part = N1 // tparts
    for start in range(0, N2, 128):
        lanes = slice(start, start + 128)
        xs = [
            series[a // per_part, :, pl.ds((a % per_part) * N2 + start, 128)] for a in range(N1)
        ]
        bins = real_fft(xs)
        for k1 in range(N1):
            if k1 <= N1 // 2:
                re, im = bins[k1]
            else:
                re, im = bins[N1 - k1]
                im = -im
            c, s = tables[k1 : k1 + 1, lanes], tables[N1 + k1 : N1 + k1 + 1, lanes]
            if im is None:
                new = re * c, -re * s
            else:
                new = re * c + im * s, im * c - re * s
            at = slice(k1 * channels, (k1 + 1) * channels)
            rows[at, start : start + 128] = new[0]
            rows[at, N2 + start : N2 + start + 128] = new[1]
    chunk = 128
    for start in range(0, N1 * channels, chunk):
        left, left_low = split_bf16(rows[start : start + chunk, :])
        total = jnp.dot(left, high[...], preferred_element_type=jnp.float32)
        total += jnp.dot(left_low, high[...], preferred_element_type=jnp.float32)
        total += jnp.dot(left, low[...], preferred_element_type=jnp.float32)
        spec[start : start + chunk, :] = total

    def parts(k1):
        at = slice(k1 * channels, (k1 + 1) * channels)
        return spec[at, :K2], spec[at, K2:]

    amplitude = []
    for k1 in range(N1):
        re, im = parts(k1)
        amplitude.append(jnp.sqrt(re * re + im * im))
    suffix = [None] * N1
    running = None
    for k1 in reversed(range(N1)):
        running = add(running, amplitude[k1])
        suffix[k1] = running
    column = running
    lane = lax.broadcasted_iota(jnp.int32, (channels, K2), 1)
    prefix = None
    for k1 in range(N1):
        prefix = add(prefix, amplitude[k1])
        above = jnp.where(lane == K2 - 1, 0.0, pltpu.roll(prefix, K2 - 1, 1))
        below = jnp.where(lane == 0, 0.0, pltpu.roll(suffix[k1], 1, 1))
        divisor = (column + above + below) / (2 * W + 1) + EPS
        scale = alive[...] / divisor
        re, im = parts(k1)
        out[k1] = jnp.concatenate([re * scale, im * scale], axis=0).astype(jnp.bfloat16)


def spectrum(blocks, alive, tables):
    tparts = lax.axis_size("ta")
    channels, time_rows = blocks[0].shape
    vmem = pl.BlockSpec(memory_space=pltpu.VMEM)
    return pl.pallas_call(
        lambda *refs: spectrum_kernel(tparts, *refs),
        out_shape=jax.ShapeDtypeStruct((N1, 2 * channels, K2), jnp.bfloat16),
        in_specs=[vmem] * (tparts + 2),
        out_specs=vmem,
        scratch_shapes=[
            pltpu.VMEM((tparts, channels, time_rows), jnp.float32),
            pltpu.VMEM((N1 * channels, 2 * N2), jnp.float32),
            pltpu.VMEM((N1 * channels, 2 * K2), jnp.float32),
            pltpu.VMEM((2 * N2, 2 * K2), jnp.bfloat16),
            pltpu.VMEM((2 * N2, 2 * K2), jnp.bfloat16),
        ],
        compiler_params=pltpu.CompilerParams(vmem_limit_bytes=32 * 1024 * 1024),
        cost_estimate=pl.CostEstimate(flops=10**9, bytes_accessed=10**6, transcendentals=10**5),
        name="spectrum",
    )(*blocks, alive, tables)


GROUP = 8


def correlate_kernel(tparts, panels, *rest):
    residents = rest[:tparts]
    table = rest[tparts]
    outs = rest[tparts + 1 : 2 * tparts + 1]
    cross, total = rest[2 * tparts + 1 :]
    steps, _, rows2, _ = panels.shape
    channels = rows2 // 2
    local = tparts * channels
    me = lax.axis_index("ta")
    total[...] = jnp.zeros_like(total)

    @pl.loop(0, N1 // GROUP)
    def _(group):
        for sub_index in range(GROUP):
            k1 = group * GROUP + sub_index
            col = sub_index * 2 * K2
            halves = [r[k1].astype(jnp.float32) for r in residents]
            re = jnp.concatenate([v[:channels] for v in halves], axis=0).astype(jnp.bfloat16)
            im = jnp.concatenate([v[channels:] for v in halves], axis=0).astype(jnp.bfloat16)
            for s in range(steps):
                panel = panels[s, k1].astype(jnp.float32)
                for i in range(channels):
                    a = jnp.broadcast_to(panel[i : i + 1, :], (local, K2)).astype(jnp.bfloat16)
                    b = jnp.broadcast_to(
                        panel[channels + i : channels + i + 1, :], (local, K2)
                    ).astype(jnp.bfloat16)
                    at = pl.ds((s * channels + i) * local, local)
                    cross[at, pl.ds(col, K2)] = a * re + b * im
                    cross[at, pl.ds(col + K2, K2)] = a * im - b * re
        depth = GROUP * 2 * K2
        total[...] += jnp.dot(
            cross[...],
            table[pl.ds(pl.multiple_of(group * depth, depth), depth), :],
            preferred_element_type=jnp.float32,
        )

    width = LAGS // tparts
    lane = lax.broadcasted_iota(jnp.int32, (channels, LAGS), 1) // width
    for source in range(0, steps * channels, 2):
        for far in range(tparts):
            dest = me ^ far
            pair = []
            for first in (source * local, (source + 1) * local):
                value = None
                for step in range(tparts):
                    at = first + step * channels
                    moved = pltpu.roll(
                        total[at : at + channels, :], (step - dest + tparts) * width % LAGS, 1
                    )
                    value = moved if value is None else jnp.where(lane == step, moved, value)
                pair.append(value)
            outs[far][source * channels : (source + 2) * channels, :] = jnp.concatenate(
                pair, axis=0
            ).astype(outs[far].dtype)


def correlate(panels, residents):
    tparts = lax.axis_size("ta")
    steps, _, rows2, _ = panels.shape
    channels = rows2 // 2
    vmem = pl.BlockSpec(memory_space=pltpu.VMEM)
    pairs = steps * channels * channels * tparts
    return pl.pallas_call(
        lambda *refs: correlate_kernel(tparts, *refs),
        out_shape=[
            jax.ShapeDtypeStruct((steps * channels * channels, LAGS), jnp.bfloat16)
        ] * tparts,
        in_specs=[vmem] * (tparts + 2),
        out_specs=[vmem] * tparts,
        scratch_shapes=[
            pltpu.VMEM((pairs, GROUP * 2 * K2), jnp.bfloat16),
            pltpu.VMEM((pairs, LAGS), jnp.float32),
        ],
        compiler_params=pltpu.CompilerParams(vmem_limit_bytes=32 * 1024 * 1024),
        cost_estimate=pl.CostEstimate(flops=4 * 10**9, bytes_accessed=3 * 10**6, transcendentals=0),
        name="correlate",
    )(panels, *residents, lag_table())


def place_kernel(tparts, steps, channels, *refs):
    pieces, out = refs[:tparts], refs[tparts]
    me = lax.axis_index("ta")
    width = LAGS // tparts
    for far in range(tparts):
        source = me ^ far
        value = pieces[far][...].astype(jnp.float32)
        for step in range(tparts):
            block = source ^ step
            moved = value if step == 0 else pltpu.roll(value, LAGS - step * width, 1)
            moved = moved[:, :width].reshape(steps, channels, channels, width)
            out[
                :,
                pl.ds(source * channels, channels),
                pl.ds(pl.multiple_of(block * channels, channels), channels),
                :,
            ] = moved


def place(pieces, steps, channels):
    tparts = lax.axis_size("ta")
    vmem = pl.BlockSpec(memory_space=pltpu.VMEM)
    local = tparts * channels
    return pl.pallas_call(
        lambda *refs: place_kernel(tparts, steps, channels, *refs),
        out_shape=jax.ShapeDtypeStruct((steps, local, local, LAGS // tparts), jnp.float32),
        in_specs=[vmem] * tparts,
        out_specs=vmem,
        compiler_params=pltpu.CompilerParams(vmem_limit_bytes=32 * 1024 * 1024),
        name="place",
    )(*pieces)


def flip(axis, mask):
    return [(i, i ^ mask) for i in range(lax.axis_size(axis))]


def exchange(block, owners):
    count, tparts = lax.axis_size("ch"), lax.axis_size("ta")
    steps = owners.shape[0]
    me = lax.axis_index("ch")
    odd = (me & 1) != 0
    if count & (count - 1) or count < 8 or tparts != 4:
        residents = [lax.ppermute(block, "ta", flip("ta", far)) for far in range(1, tparts)]
        return jnp.take(lax.all_gather(block, "ch"), owners, axis=0), residents
    away = (owners ^ me).reshape((steps,) + (1,) * block.ndim)
    held = jnp.broadcast_to(block[None], (steps,) + block.shape)
    residents = [None] * (tparts - 1)
    for far, mask in ((3, 6), (2, 4), (1, 2)):
        got = []
        for parity in (0, 1):
            perm = []
            for ch in range(count):
                for ta in range(tparts):
                    if ch & 1 == parity:
                        perm.append((ch * tparts + ta, ch * tparts + (ta ^ far)))
                    else:
                        perm.append((ch * tparts + ta, (ch ^ mask) * tparts + ta))
            got.append(lax.ppermute(block, ("ch", "ta"), perm))
        residents[far - 1] = jnp.where(odd, got[1], got[0])
        held = jnp.where((away & 6) == mask, jnp.where(odd, got[0], got[1])[None], held)
    for bit in [*range(3, count.bit_length() - 1), 0]:
        other = lax.ppermute(held, "ch", flip("ch", 1 << bit))
        held = jnp.where((away & (1 << bit)) != 0, other, held)
    return held, residents


def body(samples, dead_mask, owners):
    tparts = lax.axis_size("ta")
    me = lax.axis_index("ta")
    channels = samples.shape[0] // tparts
    steps = owners.shape[0]
    own = [
        lax.dynamic_slice_in_dim(samples, (me ^ far) * channels, channels, 0)
        for far in range(tparts)
    ]
    blocks = [own[0]] + [
        lax.ppermute(own[far], "ta", flip("ta", far)) for far in range(1, tparts)
    ]
    mask = lax.dynamic_slice_in_dim(dead_mask, me * channels, channels, 0)
    alive = jnp.broadcast_to(mask.astype(jnp.float32)[:, None], (channels, K2))
    tables = jnp.asarray(fft_tables()) * lax.optimization_barrier(jnp.float32(1))
    whitened = spectrum(blocks, alive, tables)
    panels, others = exchange(whitened, owners)
    pieces = correlate(panels, [whitened] + others)
    pieces = [pieces[0]] + [
        lax.ppermute(pieces[far], "ta", flip("ta", far)) for far in range(1, tparts)
    ]
    return place(pieces, steps, channels)


def solution(mesh):
    return jax.shard_map(
        body,
        mesh=mesh,
        in_specs=(P("ch", "ta"), P("ch"), P()),
        out_specs=P(None, None, "ch", "ta"),
        check_vma=False,
    )
```

```python
import math

import jax
import jax.numpy as jnp
import numpy as np
from jax import lax
from jax.experimental import pallas as pl
from jax.experimental.pallas import tpu as pltpu
from jax.sharding import PartitionSpec as P

NT = 8192
BINS = NT // 2
W = 32
LAGS = 128
EPS = 1e-06

N1 = 32
N2 = 256
K2 = BINS // N1
assert N1 == W and K2 == 128


SUMS_PLAN = (0, 2, 3, 1)


def split_bf16(x):
    high = x.astype(jnp.bfloat16)
    low = (x - high.astype(jnp.float32)).astype(jnp.bfloat16)
    return high, low


def fft_tables():
    twiddle = 2.0 * np.pi * (np.outer(np.arange(N1), np.arange(N2)) % NT) / NT
    angle = 2.0 * np.pi * (np.outer(np.arange(N2), np.arange(K2)) % N2) / N2
    cos, sin = np.cos(angle), np.sin(angle)
    columns = np.block([[cos, -sin], [sin, cos]])
    return np.concatenate([np.cos(twiddle), np.sin(twiddle), columns]).astype(np.float32)


def lag_table():
    k = np.arange(N1)[:, None] + N1 * np.arange(K2)[None, :]
    turns = (k[:, :, None] * ((np.arange(LAGS) - LAGS // 2) % NT)) % NT
    angle = 2.0 * np.pi * turns / NT
    table = np.stack([np.cos(angle), np.sin(angle)], axis=1) / math.sqrt(BINS)
    return table.reshape(N1 * 2 * K2, LAGS).astype(jnp.bfloat16)


def add(x, y):
    return y if x is None else x if y is None else x + y


def sub(x, y):
    return (None if y is None else -y) if x is None else x if y is None else x - y


def times(z, turn):
    re, im = z
    turn = turn % 1.0
    if turn == 0.0:
        return z
    if turn == 0.25:
        return im, None if re is None else -re
    cos, sin = math.cos(2 * math.pi * turn), math.sin(2 * math.pi * turn)
    if im is None:
        return re * cos, re * -sin
    return re * cos + im * sin, im * cos - re * sin


def real_fft(xs):
    n = len(xs)
    if n == 1:
        return [(xs[0], None)]
    if n == 2:
        return [(xs[0] + xs[1], None), (xs[0] - xs[1], None)]
    even, odd = real_fft(xs[0::2]), real_fft(xs[1::2])
    half = n // 2
    out = [None] * (half + 1)
    for k in range(half // 2 + 1):
        e, o = even[k], times(odd[k], k / n)
        out[k] = (add(e[0], o[0]), add(e[1], o[1]))
        re, im = sub(e[0], o[0]), sub(o[1], e[1])
        if k != half - k:
            out[half - k] = (re, im)
    return out


def spectrum_kernel(tparts, *rest):
    blocks = rest[:tparts]
    alive, tables, out, series, rows, spec, high, low = rest[tparts:]
    me = lax.axis_index("ta")
    channels = out.shape[1] // 2
    for step in range(tparts):
        series[me ^ step] = blocks[step][...]
    high[...], low[...] = split_bf16(tables[2 * N1 :, :])
    per_part = N1 // tparts
    for start in range(0, N2, 128):
        lanes = slice(start, start + 128)
        xs = [
            series[a // per_part, :, pl.ds((a % per_part) * N2 + start, 128)] for a in range(N1)
        ]
        bins = real_fft(xs)
        for k1 in range(N1):
            if k1 <= N1 // 2:
                re, im = bins[k1]
            else:
                re, im = bins[N1 - k1]
                im = -im
            c, s = tables[k1 : k1 + 1, lanes], tables[N1 + k1 : N1 + k1 + 1, lanes]
            if im is None:
                new = re * c, -re * s
            else:
                new = re * c + im * s, im * c - re * s
            at = slice(k1 * channels, (k1 + 1) * channels)
            rows[at, start : start + 128] = new[0]
            rows[at, N2 + start : N2 + start + 128] = new[1]
    chunk = 128
    for start in range(0, N1 * channels, chunk):
        left, left_low = split_bf16(rows[start : start + chunk, :])
        total = jnp.dot(left, high[...], preferred_element_type=jnp.float32)
        total += jnp.dot(left_low, high[...], preferred_element_type=jnp.float32)
        total += jnp.dot(left, low[...], preferred_element_type=jnp.float32)
        spec[start : start + chunk, :] = total

    def parts(k1):
        at = slice(k1 * channels, (k1 + 1) * channels)
        return spec[at, :K2], spec[at, K2:]

    amplitude = []
    for k1 in range(N1):
        re, im = parts(k1)
        amplitude.append(jnp.sqrt(re * re + im * im))
    suffix = [None] * N1
    running = None
    for k1 in reversed(range(N1)):
        running = add(running, amplitude[k1])
        suffix[k1] = running
    column = running
    lane = lax.broadcasted_iota(jnp.int32, (channels, K2), 1)
    prefix = None
    for k1 in range(N1):
        prefix = add(prefix, amplitude[k1])
        above = jnp.where(lane == K2 - 1, 0.0, pltpu.roll(prefix, K2 - 1, 1))
        below = jnp.where(lane == 0, 0.0, pltpu.roll(suffix[k1], 1, 1))
        divisor = (column + above + below) / (2 * W + 1) + EPS
        scale = alive[...] / divisor
        re, im = parts(k1)
        out[k1] = jnp.concatenate([re * scale, im * scale], axis=0).astype(jnp.bfloat16)


def spectrum(blocks, alive, tables):
    tparts = lax.axis_size("ta")
    channels, time_rows = blocks[0].shape
    vmem = pl.BlockSpec(memory_space=pltpu.VMEM)
    return pl.pallas_call(
        lambda *refs: spectrum_kernel(tparts, *refs),
        out_shape=jax.ShapeDtypeStruct((N1, 2 * channels, K2), jnp.bfloat16),
        in_specs=[vmem] * (tparts + 2),
        out_specs=vmem,
        scratch_shapes=[
            pltpu.VMEM((tparts, channels, time_rows), jnp.float32),
            pltpu.VMEM((N1 * channels, 2 * N2), jnp.float32),
            pltpu.VMEM((N1 * channels, 2 * K2), jnp.float32),
            pltpu.VMEM((2 * N2, 2 * K2), jnp.bfloat16),
            pltpu.VMEM((2 * N2, 2 * K2), jnp.bfloat16),
        ],
        compiler_params=pltpu.CompilerParams(vmem_limit_bytes=32 * 1024 * 1024),
        cost_estimate=pl.CostEstimate(flops=10**9, bytes_accessed=10**6, transcendentals=10**5),
        name="spectrum",
    )(*blocks, alive, tables)


GROUP = 8


def correlate_kernel(tparts, panels, *rest):
    residents = rest[:tparts]
    table = rest[tparts]
    outs = rest[tparts + 1 : 2 * tparts + 1]
    cross, total = rest[2 * tparts + 1 :]
    steps, _, rows2, _ = panels.shape
    channels = rows2 // 2
    local = tparts * channels
    me = lax.axis_index("ta")
    total[...] = jnp.zeros_like(total)

    @pl.loop(0, N1 // GROUP)
    def _(group):
        for sub_index in range(GROUP):
            k1 = group * GROUP + sub_index
            col = sub_index * 2 * K2
            halves = [r[k1].astype(jnp.float32) for r in residents]
            re = jnp.concatenate([v[:channels] for v in halves], axis=0).astype(jnp.bfloat16)
            im = jnp.concatenate([v[channels:] for v in halves], axis=0).astype(jnp.bfloat16)
            for s in range(steps):
                panel = panels[s, k1].astype(jnp.float32)
                for i in range(channels):
                    a = jnp.broadcast_to(panel[i : i + 1, :], (local, K2)).astype(jnp.bfloat16)
                    b = jnp.broadcast_to(
                        panel[channels + i : channels + i + 1, :], (local, K2)
                    ).astype(jnp.bfloat16)
                    at = pl.ds((s * channels + i) * local, local)
                    cross[at, pl.ds(col, K2)] = a * re + b * im
                    cross[at, pl.ds(col + K2, K2)] = a * im - b * re
        depth = GROUP * 2 * K2
        total[...] += jnp.dot(
            cross[...],
            table[pl.ds(pl.multiple_of(group * depth, depth), depth), :],
            preferred_element_type=jnp.float32,
        )

    width = LAGS // tparts
    lane = lax.broadcasted_iota(jnp.int32, (channels, LAGS), 1) // width
    for source in range(0, steps * channels, 2):
        for far in range(tparts):
            dest = me ^ SUMS_PLAN[far]
            pair = []
            for first in (source * local, (source + 1) * local):
                value = None
                for step in range(tparts):
                    at = first + step * channels
                    moved = pltpu.roll(
                        total[at : at + channels, :], (step - dest + tparts) * width % LAGS, 1
                    )
                    value = moved if value is None else jnp.where(lane == step, moved, value)
                pair.append(value)
            outs[far][source * channels : (source + 2) * channels, :] = jnp.concatenate(
                pair, axis=0
            ).astype(outs[far].dtype)


def correlate(panels, residents):
    tparts = lax.axis_size("ta")
    steps, _, rows2, _ = panels.shape
    channels = rows2 // 2
    vmem = pl.BlockSpec(memory_space=pltpu.VMEM)
    pairs = steps * channels * channels * tparts
    return pl.pallas_call(
        lambda *refs: correlate_kernel(tparts, *refs),
        out_shape=[
            jax.ShapeDtypeStruct((steps * channels * channels, LAGS), jnp.bfloat16)
        ] * tparts,
        in_specs=[vmem] * (tparts + 2),
        out_specs=[vmem] * tparts,
        scratch_shapes=[
            pltpu.VMEM((pairs, GROUP * 2 * K2), jnp.bfloat16),
            pltpu.VMEM((pairs, LAGS), jnp.float32),
        ],
        compiler_params=pltpu.CompilerParams(vmem_limit_bytes=32 * 1024 * 1024),
        cost_estimate=pl.CostEstimate(flops=4 * 10**9, bytes_accessed=3 * 10**6, transcendentals=0),
        name="correlate",
    )(panels, *residents, lag_table())


def place_kernel(tparts, steps, channels, *refs):
    pieces, out = refs[:tparts], refs[tparts]
    me = lax.axis_index("ta")
    width = LAGS // tparts
    for far in range(tparts):
        source = me ^ SUMS_PLAN[far]
        value = pieces[far][...].astype(jnp.float32)
        for step in range(tparts):
            block = source ^ step
            moved = value if step == 0 else pltpu.roll(value, LAGS - step * width, 1)
            moved = moved[:, :width].reshape(steps, channels, channels, width)
            out[
                :,
                pl.ds(source * channels, channels),
                pl.ds(pl.multiple_of(block * channels, channels), channels),
                :,
            ] = moved


def place(pieces, steps, channels):
    tparts = lax.axis_size("ta")
    vmem = pl.BlockSpec(memory_space=pltpu.VMEM)
    local = tparts * channels
    return pl.pallas_call(
        lambda *refs: place_kernel(tparts, steps, channels, *refs),
        out_shape=jax.ShapeDtypeStruct((steps, local, local, LAGS // tparts), jnp.float32),
        in_specs=[vmem] * tparts,
        out_specs=vmem,
        compiler_params=pltpu.CompilerParams(vmem_limit_bytes=32 * 1024 * 1024),
        name="place",
    )(*pieces)


def flip(axis, mask):
    return [(i, i ^ mask) for i in range(lax.axis_size(axis))]


def exchange(block, owners):
    count, tparts = lax.axis_size("ch"), lax.axis_size("ta")
    steps = owners.shape[0]
    me = lax.axis_index("ch")
    odd = (me & 1) != 0
    if count & (count - 1) or count < 8 or tparts != 4:
        residents = [lax.ppermute(block, "ta", flip("ta", far)) for far in range(1, tparts)]
        return jnp.take(lax.all_gather(block, "ch"), owners, axis=0), residents
    away = (owners ^ me).reshape((steps,) + (1,) * block.ndim)
    even_plan = [('ta', 3), ('ta', 2), ('ch', 2), ('ch', 4), ('ta', 1), ('ch', 6)]
    odd_plan = [('ch', 2), ('ch', 4), ('ta', 3), ('ta', 2), ('ch', 6), ('ta', 1)]
    got = []
    for even_move, odd_move in zip(even_plan, odd_plan):
        perm = []
        for ch in range(count):
            axis, mask = odd_move if ch & 1 else even_move
            for ta in range(tparts):
                to = (ch, ta ^ mask) if axis == "ta" else (ch ^ mask, ta)
                perm.append((ch * tparts + ta, to[0] * tparts + to[1]))
        got.append(lax.ppermute(block, ("ch", "ta"), perm))

    def result(move):
        first, second = got[even_plan.index(move)], got[odd_plan.index(move)]
        return first if first is second else jnp.where(odd, second, first)

    residents = [result(("ta", far)) for far in range(1, tparts)]
    held = jnp.broadcast_to(block[None], (steps,) + block.shape)
    for mask in (2, 4, 6):
        held = jnp.where((away & 6) == mask, result(("ch", mask))[None], held)
    for bit in [*range(3, count.bit_length() - 1), 0]:
        other = lax.ppermute(held, "ch", flip("ch", 1 << bit))
        held = jnp.where((away & (1 << bit)) != 0, other, held)
    return held, residents


def body(samples, dead_mask, owners):
    tparts = lax.axis_size("ta")
    me = lax.axis_index("ta")
    channels = samples.shape[0] // tparts
    steps = owners.shape[0]
    own = [
        lax.dynamic_slice_in_dim(samples, (me ^ far) * channels, channels, 0)
        for far in range(tparts)
    ]
    blocks = [own[0]] + [
        lax.ppermute(own[far], "ta", flip("ta", far)) for far in range(1, tparts)
    ]
    mask = lax.dynamic_slice_in_dim(dead_mask, me * channels, channels, 0)
    alive = jnp.broadcast_to(mask.astype(jnp.float32)[:, None], (channels, K2))
    tables = jnp.asarray(fft_tables()) * lax.optimization_barrier(jnp.float32(1))
    whitened = spectrum(blocks, alive, tables)
    panels, others = exchange(whitened, owners)
    pieces = correlate(panels, [whitened] + others)
    pieces = [pieces[0]] + [
        lax.ppermute(piece, "ta", flip("ta", far))
        for piece, far in zip(pieces[1:], SUMS_PLAN[1:])
    ]
    return place(pieces, steps, channels)


def solution(mesh):
    return jax.shard_map(
        body,
        mesh=mesh,
        in_specs=(P("ch", "ta"), P("ch"), P()),
        out_specs=P(None, None, "ch", "ta"),
        check_vma=False,
    )
```

```python
import math

import jax
import jax.numpy as jnp
import numpy as np
from jax import lax
from jax.experimental import pallas as pl
from jax.experimental.pallas import tpu as pltpu
from jax.sharding import PartitionSpec as P

NT = 8192
BINS = NT // 2
W = 32
LAGS = 128
EPS = 1e-06

N1 = 32
N2 = 256
K2 = BINS // N1
assert N1 == W and K2 == 128


SUMS_PLAN = (0, 2, 3, 1)


def split_bf16(x):
    high = x.astype(jnp.bfloat16)
    low = (x - high.astype(jnp.float32)).astype(jnp.bfloat16)
    return high, low


def fft_tables():
    twiddle = 2.0 * np.pi * (np.outer(np.arange(N1), np.arange(N2)) % NT) / NT
    angle = 2.0 * np.pi * (np.outer(np.arange(N2), np.arange(K2)) % N2) / N2
    cos, sin = np.cos(angle), np.sin(angle)
    columns = np.block([[cos, -sin], [sin, cos]])
    return np.concatenate([np.cos(twiddle), np.sin(twiddle), columns]).astype(np.float32)


def lag_table():
    k = np.arange(N1)[:, None] + N1 * np.arange(K2)[None, :]
    turns = (k[:, :, None] * ((np.arange(LAGS) - LAGS // 2) % NT)) % NT
    angle = 2.0 * np.pi * turns / NT
    table = np.stack([np.cos(angle), np.sin(angle)], axis=1) / math.sqrt(BINS)
    return table.reshape(N1 * 2 * K2, LAGS).astype(jnp.bfloat16)


def add(x, y):
    return y if x is None else x if y is None else x + y


def sub(x, y):
    return (None if y is None else -y) if x is None else x if y is None else x - y


def times(z, turn):
    re, im = z
    turn = turn % 1.0
    if turn == 0.0:
        return z
    if turn == 0.25:
        return im, None if re is None else -re
    cos, sin = math.cos(2 * math.pi * turn), math.sin(2 * math.pi * turn)
    if im is None:
        return re * cos, re * -sin
    return re * cos + im * sin, im * cos - re * sin


def real_fft(xs):
    n = len(xs)
    if n == 1:
        return [(xs[0], None)]
    if n == 2:
        return [(xs[0] + xs[1], None), (xs[0] - xs[1], None)]
    even, odd = real_fft(xs[0::2]), real_fft(xs[1::2])
    half = n // 2
    out = [None] * (half + 1)
    for k in range(half // 2 + 1):
        e, o = even[k], times(odd[k], k / n)
        out[k] = (add(e[0], o[0]), add(e[1], o[1]))
        re, im = sub(e[0], o[0]), sub(o[1], e[1])
        if k != half - k:
            out[half - k] = (re, im)
    return out


def spectrum_kernel(tparts, *rest):
    blocks = rest[:tparts]
    alive, tables, out, series, rows, spec, high, low = rest[tparts:]
    me = lax.axis_index("ta")
    channels = out.shape[1] // 2
    for step in range(tparts):
        series[me ^ step] = blocks[step][...]
    high[...], low[...] = split_bf16(tables[2 * N1 :, :])
    per_part = N1 // tparts
    for start in range(0, N2, 128):
        lanes = slice(start, start + 128)
        xs = [
            series[a // per_part, :, pl.ds((a % per_part) * N2 + start, 128)] for a in range(N1)
        ]
        bins = real_fft(xs)
        for k1 in range(N1):
            if k1 <= N1 // 2:
                re, im = bins[k1]
            else:
                re, im = bins[N1 - k1]
                im = -im
            c, s = tables[k1 : k1 + 1, lanes], tables[N1 + k1 : N1 + k1 + 1, lanes]
            if im is None:
                new = re * c, -re * s
            else:
                new = re * c + im * s, im * c - re * s
            at = slice(k1 * channels, (k1 + 1) * channels)
            rows[at, start : start + 128] = new[0]
            rows[at, N2 + start : N2 + start + 128] = new[1]
    chunk = 128
    for start in range(0, N1 * channels, chunk):
        left, left_low = split_bf16(rows[start : start + chunk, :])
        total = jnp.dot(left, high[...], preferred_element_type=jnp.float32)
        total += jnp.dot(left_low, high[...], preferred_element_type=jnp.float32)
        total += jnp.dot(left, low[...], preferred_element_type=jnp.float32)
        spec[start : start + chunk, :] = total

    def parts(k1):
        at = slice(k1 * channels, (k1 + 1) * channels)
        return spec[at, :K2], spec[at, K2:]

    amplitude = []
    for k1 in range(N1):
        re, im = parts(k1)
        amplitude.append(jnp.sqrt(re * re + im * im))
    suffix = [None] * N1
    running = None
    for k1 in reversed(range(N1)):
        running = add(running, amplitude[k1])
        suffix[k1] = running
    column = running
    lane = lax.broadcasted_iota(jnp.int32, (channels, K2), 1)
    prefix = None
    for k1 in range(N1):
        prefix = add(prefix, amplitude[k1])
        above = jnp.where(lane == K2 - 1, 0.0, pltpu.roll(prefix, K2 - 1, 1))
        below = jnp.where(lane == 0, 0.0, pltpu.roll(suffix[k1], 1, 1))
        divisor = (column + above + below) / (2 * W + 1) + EPS
        scale = alive[...] / divisor
        re, im = parts(k1)
        out[k1] = jnp.concatenate([re * scale, im * scale], axis=0).astype(jnp.bfloat16)


def spectrum(blocks, alive, tables):
    tparts = lax.axis_size("ta")
    channels, time_rows = blocks[0].shape
    vmem = pl.BlockSpec(memory_space=pltpu.VMEM)
    return pl.pallas_call(
        lambda *refs: spectrum_kernel(tparts, *refs),
        out_shape=jax.ShapeDtypeStruct((N1, 2 * channels, K2), jnp.bfloat16),
        in_specs=[vmem] * (tparts + 2),
        out_specs=vmem,
        scratch_shapes=[
            pltpu.VMEM((tparts, channels, time_rows), jnp.float32),
            pltpu.VMEM((N1 * channels, 2 * N2), jnp.float32),
            pltpu.VMEM((N1 * channels, 2 * K2), jnp.float32),
            pltpu.VMEM((2 * N2, 2 * K2), jnp.bfloat16),
            pltpu.VMEM((2 * N2, 2 * K2), jnp.bfloat16),
        ],
        compiler_params=pltpu.CompilerParams(vmem_limit_bytes=32 * 1024 * 1024),
        cost_estimate=pl.CostEstimate(flops=10**9, bytes_accessed=10**6, transcendentals=10**5),
        name="spectrum",
    )(*blocks, alive, tables)


GROUPS = (2, 6, 12, 12)


def correlate_kernel(tparts, panels, *rest):
    residents = rest[:tparts]
    table = rest[tparts]
    outs = rest[tparts + 1 : 2 * tparts + 1]
    *crosses, total = rest[2 * tparts + 1 :]
    steps, _, rows2, _ = panels.shape
    channels = rows2 // 2
    local = tparts * channels
    me = lax.axis_index("ta")
    starts = [sum(GROUPS[:index]) for index in range(len(GROUPS) + 1)]

    def fill(cross, group):
        for k1 in range(starts[group], starts[group + 1]):
            col = (k1 - starts[group]) * 2 * K2
            halves = [r[k1].astype(jnp.float32) for r in residents]
            re = jnp.concatenate([v[:channels] for v in halves], axis=0).astype(jnp.bfloat16)
            im = jnp.concatenate([v[channels:] for v in halves], axis=0).astype(jnp.bfloat16)
            for s in range(steps):
                panel = panels[s, k1].astype(jnp.float32)
                for i in range(channels):
                    a = jnp.broadcast_to(panel[i : i + 1, :], (local, K2)).astype(jnp.bfloat16)
                    b = jnp.broadcast_to(
                        panel[channels + i : channels + i + 1, :], (local, K2)
                    ).astype(jnp.bfloat16)
                    at = pl.ds((s * channels + i) * local, local)
                    cross[at, pl.ds(col, K2)] = a * re + b * im
                    cross[at, pl.ds(col + K2, K2)] = a * im - b * re

    fill(crosses[0], 0)
    for group in range(len(GROUPS)):
        if group + 1 < len(GROUPS):
            fill(crosses[group + 1], group + 1)
        part = jnp.dot(
            crosses[group][...],
            table[starts[group] * 2 * K2 : starts[group + 1] * 2 * K2, :],
            preferred_element_type=jnp.float32,
        )
        if group == 0:
            total[...] = part
        else:
            total[...] += part

    width = LAGS // tparts
    lane = lax.broadcasted_iota(jnp.int32, (channels, LAGS), 1) // width
    for source in range(0, steps * channels, 2):
        for far in range(tparts):
            dest = me ^ SUMS_PLAN[far]
            pair = []
            for first in (source * local, (source + 1) * local):
                value = None
                for step in range(tparts):
                    at = first + step * channels
                    moved = pltpu.roll(
                        total[at : at + channels, :], (step - dest + tparts) * width % LAGS, 1
                    )
                    value = moved if value is None else jnp.where(lane == step, moved, value)
                pair.append(value)
            outs[far][source * channels : (source + 2) * channels, :] = jnp.concatenate(
                pair, axis=0
            ).astype(outs[far].dtype)


def correlate(panels, residents):
    tparts = lax.axis_size("ta")
    steps, _, rows2, _ = panels.shape
    channels = rows2 // 2
    vmem = pl.BlockSpec(memory_space=pltpu.VMEM)
    pairs = steps * channels * channels * tparts
    return pl.pallas_call(
        lambda *refs: correlate_kernel(tparts, *refs),
        out_shape=[
            jax.ShapeDtypeStruct((steps * channels * channels, LAGS), jnp.bfloat16)
        ] * tparts,
        in_specs=[vmem] * (tparts + 2),
        out_specs=[vmem] * tparts,
        scratch_shapes=[
            pltpu.VMEM((pairs, group * 2 * K2), jnp.bfloat16) for group in GROUPS
        ]
        + [pltpu.VMEM((pairs, LAGS), jnp.float32)],
        compiler_params=pltpu.CompilerParams(vmem_limit_bytes=32 * 1024 * 1024),
        cost_estimate=pl.CostEstimate(flops=4 * 10**9, bytes_accessed=3 * 10**6, transcendentals=0),
        name="correlate",
    )(panels, *residents, lag_table())


def place_kernel(tparts, steps, channels, *refs):
    pieces, out = refs[:tparts], refs[tparts]
    me = lax.axis_index("ta")
    width = LAGS // tparts
    for far in range(tparts):
        source = me ^ SUMS_PLAN[far]
        value = pieces[far][...].astype(jnp.float32)
        for step in range(tparts):
            block = source ^ step
            moved = value if step == 0 else pltpu.roll(value, LAGS - step * width, 1)
            moved = moved[:, :width].reshape(steps, channels, channels, width)
            out[
                :,
                pl.ds(source * channels, channels),
                pl.ds(pl.multiple_of(block * channels, channels), channels),
                :,
            ] = moved


def place(pieces, steps, channels):
    tparts = lax.axis_size("ta")
    vmem = pl.BlockSpec(memory_space=pltpu.VMEM)
    local = tparts * channels
    return pl.pallas_call(
        lambda *refs: place_kernel(tparts, steps, channels, *refs),
        out_shape=jax.ShapeDtypeStruct((steps, local, local, LAGS // tparts), jnp.float32),
        in_specs=[vmem] * tparts,
        out_specs=vmem,
        compiler_params=pltpu.CompilerParams(vmem_limit_bytes=32 * 1024 * 1024),
        name="place",
    )(*pieces)


def flip(axis, mask):
    return [(i, i ^ mask) for i in range(lax.axis_size(axis))]


def exchange(block, owners):
    count, tparts = lax.axis_size("ch"), lax.axis_size("ta")
    steps = owners.shape[0]
    me = lax.axis_index("ch")
    odd = (me & 1) != 0
    if count & (count - 1) or count < 8 or tparts != 4:
        residents = [lax.ppermute(block, "ta", flip("ta", far)) for far in range(1, tparts)]
        return jnp.take(lax.all_gather(block, "ch"), owners, axis=0), residents
    away = (owners ^ me).reshape((steps,) + (1,) * block.ndim)
    even_plan = [("ta", 3), ("ta", 2), ("ta", 1), ("ch", 2), ("ch", 4), ("ch", 6)]
    odd_plan = even_plan[3:] + even_plan[:3]
    got = []
    for even_move, odd_move in zip(even_plan, odd_plan):
        perm = []
        for ch in range(count):
            axis, mask = odd_move if ch & 1 else even_move
            for ta in range(tparts):
                to = (ch, ta ^ mask) if axis == "ta" else (ch ^ mask, ta)
                perm.append((ch * tparts + ta, to[0] * tparts + to[1]))
        got.append(lax.ppermute(block, ("ch", "ta"), perm))

    def result(move):
        first, second = got[even_plan.index(move)], got[odd_plan.index(move)]
        return first if first is second else jnp.where(odd, second, first)

    residents = [result(("ta", far)) for far in range(1, tparts)]
    held = jnp.broadcast_to(block[None], (steps,) + block.shape)
    for mask in (2, 4, 6):
        held = jnp.where((away & 6) == mask, result(("ch", mask))[None], held)
    for bit in [*range(3, count.bit_length() - 1), 0]:
        other = lax.ppermute(held, "ch", flip("ch", 1 << bit))
        held = jnp.where((away & (1 << bit)) != 0, other, held)
    return held, residents


def body(samples, dead_mask, owners):
    tparts = lax.axis_size("ta")
    me = lax.axis_index("ta")
    channels = samples.shape[0] // tparts
    steps = owners.shape[0]
    own = [
        lax.dynamic_slice_in_dim(samples, (me ^ far) * channels, channels, 0)
        for far in range(tparts)
    ]
    blocks = [own[0]] + [
        lax.ppermute(own[far], "ta", flip("ta", far)) for far in range(1, tparts)
    ]
    mask = lax.dynamic_slice_in_dim(dead_mask, me * channels, channels, 0)
    alive = jnp.broadcast_to(mask.astype(jnp.float32)[:, None], (channels, K2))
    tables = jnp.asarray(fft_tables()) * lax.optimization_barrier(jnp.float32(1))
    whitened = spectrum(blocks, alive, tables)
    panels, others = exchange(whitened, owners)
    pieces = correlate(panels, [whitened] + others)
    pieces = [pieces[0]] + [
        lax.ppermute(piece, "ta", flip("ta", far))
        for piece, far in zip(pieces[1:], SUMS_PLAN[1:])
    ]
    return place(pieces, steps, channels)


def solution(mesh):
    return jax.shard_map(
        body,
        mesh=mesh,
        in_specs=(P("ch", "ta"), P("ch"), P()),
        out_specs=P(None, None, "ch", "ta"),
        check_vma=False,
    )
```

```python
import math

import jax
import jax.numpy as jnp
import numpy as np
from jax import lax
from jax.experimental import pallas as pl
from jax.experimental.pallas import tpu as pltpu
from jax.sharding import PartitionSpec as P

NT = 8192
BINS = NT // 2
W = 32
LAGS = 128
EPS = 1e-06

N1 = 32
N2 = 256
K2 = BINS // N1
assert N1 == W and K2 == 128


SUMS_PLAN = (0, 2, 3, 1)


def split_bf16(x):
    high = x.astype(jnp.bfloat16)
    low = (x - high.astype(jnp.float32)).astype(jnp.bfloat16)
    return high, low


def fft_tables():
    twiddle = 2.0 * np.pi * (np.outer(np.arange(N1), np.arange(N2)) % NT) / NT
    angle = 2.0 * np.pi * (np.outer(np.arange(N2), np.arange(K2)) % N2) / N2
    cos, sin = np.cos(angle), np.sin(angle)
    columns = np.block([[cos, -sin], [sin, cos]])
    return np.concatenate([np.cos(twiddle), np.sin(twiddle), columns]).astype(np.float32)


def lag_table():
    k = np.arange(N1)[:, None] + N1 * np.arange(K2)[None, :]
    turns = (k[:, :, None] * ((np.arange(LAGS) - LAGS // 2) % NT)) % NT
    angle = 2.0 * np.pi * turns / NT
    table = np.stack([np.cos(angle), np.sin(angle)], axis=1) / math.sqrt(BINS)
    return table.reshape(N1 * 2 * K2, LAGS).astype(jnp.bfloat16)


def add(x, y):
    return y if x is None else x if y is None else x + y


def sub(x, y):
    return (None if y is None else -y) if x is None else x if y is None else x - y


def times(z, turn):
    re, im = z
    turn = turn % 1.0
    if turn == 0.0:
        return z
    if turn == 0.25:
        return im, None if re is None else -re
    cos, sin = math.cos(2 * math.pi * turn), math.sin(2 * math.pi * turn)
    if im is None:
        return re * cos, re * -sin
    return re * cos + im * sin, im * cos - re * sin


def real_fft(xs):
    n = len(xs)
    if n == 1:
        return [(xs[0], None)]
    if n == 2:
        return [(xs[0] + xs[1], None), (xs[0] - xs[1], None)]
    even, odd = real_fft(xs[0::2]), real_fft(xs[1::2])
    half = n // 2
    out = [None] * (half + 1)
    for k in range(half // 2 + 1):
        e, o = even[k], times(odd[k], k / n)
        out[k] = (add(e[0], o[0]), add(e[1], o[1]))
        re, im = sub(e[0], o[0]), sub(o[1], e[1])
        if k != half - k:
            out[half - k] = (re, im)
    return out


def spectrum_kernel(tparts, *rest):
    blocks = rest[:tparts]
    alive, tables, out, series, rows, spec, high, low = rest[tparts:]
    me = lax.axis_index("ta")
    channels = out.shape[1] // 2
    for step in range(tparts):
        series[me ^ step] = blocks[step][...]
    high[...], low[...] = split_bf16(tables[2 * N1 :, :])
    per_part = N1 // tparts
    for start in range(0, N2, 128):
        lanes = slice(start, start + 128)
        xs = [
            series[a // per_part, :, pl.ds((a % per_part) * N2 + start, 128)] for a in range(N1)
        ]
        bins = real_fft(xs)
        for k1 in range(N1):
            if k1 <= N1 // 2:
                re, im = bins[k1]
            else:
                re, im = bins[N1 - k1]
                im = -im
            c, s = tables[k1 : k1 + 1, lanes], tables[N1 + k1 : N1 + k1 + 1, lanes]
            if im is None:
                new = re * c, -re * s
            else:
                new = re * c + im * s, im * c - re * s
            at = slice(k1 * channels, (k1 + 1) * channels)
            rows[at, start : start + 128] = new[0]
            rows[at, N2 + start : N2 + start + 128] = new[1]
    chunk = 128
    for start in range(0, N1 * channels, chunk):
        left, left_low = split_bf16(rows[start : start + chunk, :])
        total = jnp.dot(left, high[...], preferred_element_type=jnp.float32)
        total += jnp.dot(left_low, high[...], preferred_element_type=jnp.float32)
        total += jnp.dot(left, low[...], preferred_element_type=jnp.float32)
        spec[start : start + chunk, :] = total

    def parts(k1):
        at = slice(k1 * channels, (k1 + 1) * channels)
        return spec[at, :K2], spec[at, K2:]

    amplitude = []
    for k1 in range(N1):
        re, im = parts(k1)
        amplitude.append(jnp.sqrt(re * re + im * im))
    suffix = [None] * N1
    running = None
    for k1 in reversed(range(N1)):
        running = add(running, amplitude[k1])
        suffix[k1] = running
    column = running
    lane = lax.broadcasted_iota(jnp.int32, (channels, K2), 1)
    prefix = None
    for k1 in range(N1):
        prefix = add(prefix, amplitude[k1])
        above = jnp.where(lane == K2 - 1, 0.0, pltpu.roll(prefix, K2 - 1, 1))
        below = jnp.where(lane == 0, 0.0, pltpu.roll(suffix[k1], 1, 1))
        divisor = (column + above + below) / (2 * W + 1) + EPS
        scale = alive[...] / divisor
        re, im = parts(k1)
        out[k1] = jnp.concatenate([re * scale, im * scale], axis=0).astype(jnp.bfloat16)


def spectrum(blocks, alive, tables):
    tparts = lax.axis_size("ta")
    channels, time_rows = blocks[0].shape
    vmem = pl.BlockSpec(memory_space=pltpu.VMEM)
    return pl.pallas_call(
        lambda *refs: spectrum_kernel(tparts, *refs),
        out_shape=jax.ShapeDtypeStruct((N1, 2 * channels, K2), jnp.bfloat16),
        in_specs=[vmem] * (tparts + 2),
        out_specs=vmem,
        scratch_shapes=[
            pltpu.VMEM((tparts, channels, time_rows), jnp.float32),
            pltpu.VMEM((N1 * channels, 2 * N2), jnp.float32),
            pltpu.VMEM((N1 * channels, 2 * K2), jnp.float32),
            pltpu.VMEM((2 * N2, 2 * K2), jnp.bfloat16),
            pltpu.VMEM((2 * N2, 2 * K2), jnp.bfloat16),
        ],
        compiler_params=pltpu.CompilerParams(vmem_limit_bytes=32 * 1024 * 1024),
        cost_estimate=pl.CostEstimate(flops=10**9, bytes_accessed=10**6, transcendentals=10**5),
        name="spectrum",
    )(*blocks, alive, tables)


GROUPS = (1, 3, 8, 10, 10)


def correlate_kernel(tparts, panels, *rest):
    residents = rest[:tparts]
    table = rest[tparts]
    outs = rest[tparts + 1 : 2 * tparts + 1]
    *crosses, total = rest[2 * tparts + 1 :]
    steps, _, rows2, _ = panels.shape
    channels = rows2 // 2
    local = tparts * channels
    me = lax.axis_index("ta")
    starts = [sum(GROUPS[:index]) for index in range(len(GROUPS) + 1)]

    def fill(cross, group):
        for k1 in range(starts[group], starts[group + 1]):
            col = (k1 - starts[group]) * 2 * K2
            halves = [r[k1].astype(jnp.float32) for r in residents]
            re = jnp.concatenate([v[:channels] for v in halves], axis=0).astype(jnp.bfloat16)
            im = jnp.concatenate([v[channels:] for v in halves], axis=0).astype(jnp.bfloat16)
            for s in range(steps):
                panel = panels[s, k1].astype(jnp.float32)
                for i in range(channels):
                    a = jnp.broadcast_to(panel[i : i + 1, :], (local, K2)).astype(jnp.bfloat16)
                    b = jnp.broadcast_to(
                        panel[channels + i : channels + i + 1, :], (local, K2)
                    ).astype(jnp.bfloat16)
                    at = pl.ds((s * channels + i) * local, local)
                    cross[at, pl.ds(col, K2)] = a * re + b * im
                    cross[at, pl.ds(col + K2, K2)] = a * im - b * re

    fill(crosses[0], 0)
    for group in range(len(GROUPS)):
        if group + 1 < len(GROUPS):
            fill(crosses[group + 1], group + 1)
        part = jnp.dot(
            crosses[group][...],
            table[starts[group] * 2 * K2 : starts[group + 1] * 2 * K2, :],
            preferred_element_type=jnp.float32,
        )
        if group == 0:
            total[...] = part
        else:
            total[...] += part

    width = LAGS // tparts
    lane = lax.broadcasted_iota(jnp.int32, (channels, LAGS), 1) // width
    for source in range(0, steps * channels, 2):
        for far in range(tparts):
            dest = me ^ SUMS_PLAN[far]
            pair = []
            for first in (source * local, (source + 1) * local):
                value = None
                for step in range(tparts):
                    at = first + step * channels
                    moved = pltpu.roll(
                        total[at : at + channels, :], (step - dest + tparts) * width % LAGS, 1
                    )
                    value = moved if value is None else jnp.where(lane == step, moved, value)
                pair.append(value)
            outs[far][source * channels : (source + 2) * channels, :] = jnp.concatenate(
                pair, axis=0
            ).astype(outs[far].dtype)


def correlate(panels, residents):
    tparts = lax.axis_size("ta")
    steps, _, rows2, _ = panels.shape
    channels = rows2 // 2
    vmem = pl.BlockSpec(memory_space=pltpu.VMEM)
    pairs = steps * channels * channels * tparts
    return pl.pallas_call(
        lambda *refs: correlate_kernel(tparts, *refs),
        out_shape=[
            jax.ShapeDtypeStruct((steps * channels * channels, LAGS), jnp.bfloat16)
        ] * tparts,
        in_specs=[vmem] * (tparts + 2),
        out_specs=[vmem] * tparts,
        scratch_shapes=[
            pltpu.VMEM((pairs, group * 2 * K2), jnp.bfloat16) for group in GROUPS
        ]
        + [pltpu.VMEM((pairs, LAGS), jnp.float32)],
        compiler_params=pltpu.CompilerParams(vmem_limit_bytes=32 * 1024 * 1024),
        cost_estimate=pl.CostEstimate(flops=4 * 10**9, bytes_accessed=3 * 10**6, transcendentals=0),
        name="correlate",
    )(panels, *residents, lag_table())


def place_kernel(slots, steps, channels, tparts, *refs):
    count = len(slots)
    pieces = refs[:count]
    out, stage, sems = refs[-3:]
    me = lax.axis_index("ta")
    width = LAGS // tparts
    copies = []
    for index, slot in enumerate(slots):
        source = me ^ SUMS_PLAN[slot]
        value = pieces[index][...].astype(jnp.float32)
        for step in range(tparts):
            block = source ^ step
            moved = value if step == 0 else pltpu.roll(value, LAGS - step * width, 1)
            stage[index, :, :, pl.ds(pl.multiple_of(block * channels, channels), channels), :] = (
                moved[:, :width].reshape(steps, channels, channels, width)
            )
        copy = pltpu.make_async_copy(
            stage.at[index], out.at[:, pl.ds(source * channels, channels)], sems.at[index]
        )
        copy.start()
        copies.append(copy)
    for copy in copies:
        copy.wait()


def place(pieces, slots, steps, channels, held=None):
    tparts = lax.axis_size("ta")
    count = len(slots)
    vmem = pl.BlockSpec(memory_space=pltpu.VMEM)
    hbm = pl.BlockSpec(memory_space=pltpu.HBM)
    local = tparts * channels
    more = [] if held is None else [held]
    return pl.pallas_call(
        lambda *refs: place_kernel(slots, steps, channels, tparts, *refs),
        out_shape=jax.ShapeDtypeStruct((steps, local, local, LAGS // tparts), jnp.float32),
        in_specs=[vmem] * count + [hbm] * len(more),
        out_specs=hbm,
        scratch_shapes=[
            pltpu.VMEM((count, steps, channels, local, LAGS // tparts), jnp.float32),
            pltpu.SemaphoreType.DMA((count,)),
        ],
        input_output_aliases={count: 0} if more else {},
        compiler_params=pltpu.CompilerParams(vmem_limit_bytes=32 * 1024 * 1024),
        name="place",
    )(*[pieces[slot] for slot in slots], *more)


def flip(axis, mask):
    return [(i, i ^ mask) for i in range(lax.axis_size(axis))]


def exchange(block, owners):
    count, tparts = lax.axis_size("ch"), lax.axis_size("ta")
    steps = owners.shape[0]
    me = lax.axis_index("ch")
    odd = (me & 1) != 0
    if count & (count - 1) or count < 8 or tparts != 4:
        residents = [lax.ppermute(block, "ta", flip("ta", far)) for far in range(1, tparts)]
        return jnp.take(lax.all_gather(block, "ch"), owners, axis=0), residents
    away = (owners ^ me).reshape((steps,) + (1,) * block.ndim)
    even_plan = [("ta", 3), ("ta", 2), ("ta", 1), ("ch", 2), ("ch", 4), ("ch", 6)]
    odd_plan = even_plan[3:] + even_plan[:3]
    got = []
    for even_move, odd_move in zip(even_plan, odd_plan):
        perm = []
        for ch in range(count):
            axis, mask = odd_move if ch & 1 else even_move
            for ta in range(tparts):
                to = (ch, ta ^ mask) if axis == "ta" else (ch ^ mask, ta)
                perm.append((ch * tparts + ta, to[0] * tparts + to[1]))
        got.append(lax.ppermute(block, ("ch", "ta"), perm))

    def result(move):
        first, second = got[even_plan.index(move)], got[odd_plan.index(move)]
        return first if first is second else jnp.where(odd, second, first)

    residents = [result(("ta", far)) for far in range(1, tparts)]
    held = jnp.broadcast_to(block[None], (steps,) + block.shape)
    for mask in (2, 4, 6):
        held = jnp.where((away & 6) == mask, result(("ch", mask))[None], held)
    for bit in [*range(3, count.bit_length() - 1), 0]:
        other = lax.ppermute(held, "ch", flip("ch", 1 << bit))
        held = jnp.where((away & (1 << bit)) != 0, other, held)
    return held, residents


def body(samples, dead_mask, owners):
    tparts = lax.axis_size("ta")
    me = lax.axis_index("ta")
    channels = samples.shape[0] // tparts
    steps = owners.shape[0]
    own = [
        lax.dynamic_slice_in_dim(samples, (me ^ far) * channels, channels, 0)
        for far in range(tparts)
    ]
    blocks = [own[0]] + [
        lax.ppermute(own[far], "ta", flip("ta", far)) for far in range(1, tparts)
    ]
    mask = lax.dynamic_slice_in_dim(dead_mask, me * channels, channels, 0)
    alive = jnp.broadcast_to(mask.astype(jnp.float32)[:, None], (channels, K2))
    tables = jnp.asarray(fft_tables()) * lax.optimization_barrier(jnp.float32(1))
    whitened = spectrum(blocks, alive, tables)
    panels, others = exchange(whitened, owners)
    pieces = correlate(panels, [whitened] + others)
    pieces = [pieces[0]] + [
        lax.ppermute(piece, "ta", flip("ta", far))
        for piece, far in zip(pieces[1:], SUMS_PLAN[1:])
    ]
    held = place(pieces, range(2), steps, channels)
    return place(pieces, range(2, tparts), steps, channels, held)


def solution(mesh):
    return jax.shard_map(
        body,
        mesh=mesh,
        in_specs=(P("ch", "ta"), P("ch"), P()),
        out_specs=P(None, None, "ch", "ta"),
        check_vma=False,
    )
```
